1024 devices in a mesh: wide: 256 (over z, y, x_lo), narrow: 4 (over x_hi, core).
Axes of the slice: x: 4 (x_hi: 2, x_lo: 2; x = x_hi * 2 + x_lo), y: 4, z: 32, core: 2. Of those that a mesh axis runs over, the one named last changes fastest.
Arguments:
- chi_in: float32 [40960, 2048], P('wide', 'narrow'), may hold values from -6 to 6
- val_orb: float32 [40960, 4096], P(('wide', 'narrow')), may hold values from -4 to 4
- cond_orb: float32 [40960, 4096], P(('wide', 'narrow')), may hold values from -4 to 4
- e_val: float32 [4096], replicated, may hold values from -12 to -0.5
- e_cond: float32 [4096], replicated, may hold values from 0.5 to 12
- pair_val: int32 [1, 512], replicated, may hold values from 0 to 4095
- pair_cond: int32 [1, 512], replicated, may hold values from 0 to 4095
Outputs:
- chi_out: float32 [40960, 2048], P('wide', 'narrow')
The draws below stay inside these ranges and needn't reach their ends.
All inputs are finite; a program needn't handle non-finite values.
Results may differ from the reference program's by a relative error of at most 0.0001.
Values sent between devices are 32-bit elements; how exact they have to be, the bound alone decides.
A program may use at most 32 MiB of HBM per device.

```python
import jax
import jax.numpy as jnp
from jax import lax

NV = 4096
NC = 4096
PAIRS = 512
GROUPS = 1
G_DEV = 160
NG = 40960
SLAB = 2048
RSUB = 2
N_WIDE = 256


def plant(drawn, key, smallest, high):
    shape = drawn.shape
    spot = [jax.random.randint(jax.random.fold_in(key, axis), (), 0, shape[axis]) for axis in range(len(shape))]
    drawn = drawn.at[tuple(spot)].set(smallest)
    longest = shape.index(max(shape))
    spot[longest] = (spot[longest] + 1) % shape[longest]
    return drawn.at[tuple(spot)].set(high)


def shard_levels(stream_key, extent, split, low, largest):
    def one(position, shards_of):
        draws = jax.random.uniform(jax.random.fold_in(jax.random.fold_in(stream_key, 6), position), (shards_of,), jnp.float32, low / len(split), largest / len(split))
        return jnp.repeat(jnp.exp(draws), extent[position] // shards_of).reshape((-1,) + (1,) * (len(extent) - position - 1))

    loudness = one(*split[0])
    for cut in split[1:]:
        loudness = loudness * one(*cut)
    return loudness


def noise(stream_key, dims, spread, most, cuts=(), kind=jnp.bfloat16):
    gain = shard_levels(stream_key, dims, cuts, -0.22, 0.18) if cuts else 1.0
    values = jax.random.normal(stream_key, dims, jnp.float32) * spread * gain
    return jnp.minimum(jnp.maximum(values, -most), most).astype(kind)


def setup_inputs(seed: int = 0) -> dict:
    arg_keys = jax.random.split(jax.random.key(seed), 8)
    chi_in = noise(arg_keys[0], (NG, SLAB), 1.0, 6.0, ((0, 256), (1, 4)), jnp.float32)
    val_orb = noise(arg_keys[1], (NG, NV), 0.6, 4.0, ((0, 1024),), jnp.float32)
    cond_orb = noise(arg_keys[2], (NG, NC), 0.6, 4.0, ((0, 1024),), jnp.float32)
    e_val = jnp.clip(jax.random.uniform(arg_keys[3], (NV,), jnp.float32, -12.0, -0.5), -12.0, -0.5)
    e_cond = jnp.clip(jax.random.uniform(arg_keys[4], (NC,), jnp.float32, 0.5, 12.0), 0.5, 12.0)
    pair_val = plant(jax.random.randint(arg_keys[5], (GROUPS, PAIRS), 0, NV), jax.random.fold_in(arg_keys[5], 1), 0, NV - 1).astype(jnp.int32)
    pair_cond = plant(jax.random.randint(arg_keys[6], (GROUPS, PAIRS), 0, NC), jax.random.fold_in(arg_keys[6], 1), 0, NC - 1).astype(jnp.int32)
    return {"chi_in": chi_in, "val_orb": val_orb, "cond_orb": cond_orb, "e_val": e_val, "e_cond": e_cond, "pair_val": pair_val, "pair_cond": pair_cond}


def slab_points():
    rows = jnp.arange(SLAB, dtype=jnp.int32)
    per_tile = RSUB * N_WIDE
    tile = rows // per_tile
    block = (rows // RSUB) % N_WIDE
    inner = rows % RSUB
    return (block * G_DEV + tile * RSUB + inner).astype(jnp.int32)


def reference(chi_in, val_orb, cond_orb, e_val, e_cond, pair_val, pair_cond):
    points = slab_points()
    chi = chi_in
    for block in range(GROUPS):
        dens = val_orb[:, pair_val[block]] * cond_orb[:, pair_cond[block]]
        weight = 1.0 / (e_cond[pair_cond[block]] - e_val[pair_val[block]])
        rows_part = dens[points]
        weighted = dens * weight[None, :]
        chi = chi + jnp.dot(weighted, rows_part.T, precision=lax.Precision.HIGHEST, preferred_element_type=jnp.float32)
    return chi
```

```python
import functools

import jax
import jax.numpy as jnp
from jax import lax
from jax.experimental import pallas as pl
from jax.experimental.pallas import tpu as pltpu
from jax.sharding import PartitionSpec as P

MESH = pl.DeviceIdType.MESH
LANES = 128
NY = 4
NX = 2
Z_ORDER = (1, 2, 3, 8, 4, 5, 6, 7)


def kernel(
    n_wide, n_narrow, pairs, reach,
    pv_ref, pc_ref, ev_ref, ec_ref, val_ref, cond_ref, chi_ref,
    out_ref,
    pv, pc, ev, ec, vbuf, cbuf, chi, stage, slab, cols,
    in_sems, x_send, x_recv, col_send, col_recv, z_send, z_recv, far_recv, y_send, y_recv,
):
    me_w = lax.axis_index("wide")
    me_n = lax.axis_index("narrow")
    nz = n_wide // (NY * NX)
    z, y, xl = me_w // (NY * NX), (me_w // NX) % NY, me_w % NX
    groups = pairs // LANES
    unit = 2 * groups
    pair_unit = unit * NX
    points = vbuf.shape[0]
    n_x = NX * n_narrow - 1

    def wide_of(zz, yy, xx):
        return (zz * NY + yy) * NX + xx

    def dev(w, n):
        return {"wide": w, "narrow": n}

    def shift_z(dz):
        return lax.rem(z + dz + nz, nz)

    def shift_y(dy):
        return lax.rem(y + dy + NY, NY)

    small = [
        pltpu.make_async_copy(s, d, in_sems.at[i])
        for i, (s, d) in enumerate([(pv_ref, pv), (pc_ref, pc), (ev_ref, ev), (ec_ref, ec)])
    ]
    heads = [
        pltpu.make_async_copy(s.at[pl.ds(0, 8)], d.at[pl.ds(0, 8)], in_sems.at[4 + i])
        for i, (s, d) in enumerate([(val_ref, vbuf), (cond_ref, cbuf)])
    ]
    rests = [
        pltpu.make_async_copy(
            s.at[pl.ds(8, points - 8)], d.at[pl.ds(8, points - 8)], in_sems.at[6 + i]
        )
        for i, (s, d) in enumerate([(val_ref, vbuf), (cond_ref, cbuf)])
    ]
    chi_load = pltpu.make_async_copy(chi_ref, chi, in_sems.at[8])
    for c in small + heads + rests + [chi_load]:
        c.start()

    barrier = pltpu.get_barrier_semaphore()

    def greet(w, n):
        pl.semaphore_signal(barrier, inc=1, device_id=dev(w, n), device_id_type=MESH)

    for src in range(NX):
        @pl.when(jnp.logical_or(me_n != 0, xl != src))
        def _():
            greet(wide_of(z, y, src), 0)
    for k in range(1, n_narrow):
        greet(me_w, lax.rem(me_n + k, n_narrow))
    for dy in (1, 3, 2):
        greet(wide_of(z, shift_y(dy), xl), me_n)
    for dz in range(1, reach + 1):
        greet(wide_of(shift_z(dz), y, xl), me_n)
        greet(wide_of(shift_z(-dz), y, xl), me_n)
    always = (n_narrow - 1) + 3 + 2 * reach

    for c in small:
        c.wait()
    for c in heads:
        c.wait()

    def split(ref, a):
        index = jnp.broadcast_to(ref[0:1, a * LANES:(a + 1) * LANES], (8, LANES))
        return index & (LANES - 1), index >> 7

    idx_v = [split(pv, a) for a in range(groups)]
    idx_c = [split(pc, a) for a in range(groups)]
    chunks = vbuf.shape[1] // LANES

    def pick(load_v, load_c):
        def body(c, acc):
            rows_v, rows_c = load_v(c), load_c(c)
            new = []
            for a in range(groups):
                for rows, (lo, hi), old in (
                    (rows_v, idx_v[a], acc[2 * a]),
                    (rows_c, idx_c[a], acc[2 * a + 1]),
                ):
                    got = jnp.take_along_axis(rows, lo, axis=1, mode="promise_in_bounds")
                    new.append(jnp.where(hi == c, got, old))
            return tuple(new)

        zero = jnp.zeros((8, LANES), jnp.float32)
        return lax.fori_loop(0, chunks, body, (zero,) * (2 * groups))

    def density(start):
        def load(ref):
            return lambda c: ref[
                pl.ds(start, 8), pl.ds(pl.multiple_of(c * LANES, LANES), LANES)
            ]

        got = pick(load(vbuf), load(cbuf))
        return [got[2 * a] * got[2 * a + 1] for a in range(groups)]

    first = density(0)
    for a in range(groups):
        stage[pl.ds(a, 8, stride=groups), :] = first[a]
        cols[me_n, pl.ds(0, 8), a * LANES:(a + 1) * LANES] = first[a]

    home = wide_of(z, y, 0) * unit
    own = pl.ds(pl.multiple_of(home + xl * unit, 8), unit)

    @pl.when(me_n == 0)
    def _():
        slab[own, :] = stage[pl.ds(0, unit), :]
        pl.semaphore_wait(barrier, always + n_x)
        for k in range(1, NX * n_narrow):
            xx, n = lax.rem(xl + k // n_narrow, NX), k % n_narrow
            pltpu.make_async_remote_copy(
                src_ref=stage.at[pl.ds(n * unit, unit)],
                dst_ref=slab.at[own],
                send_sem=x_send,
                recv_sem=x_recv.at[xl],
                device_id=dev(wide_of(z, y, xx), n),
                device_id_type=MESH,
            ).start()

    @pl.when(me_n != 0)
    def _():
        pl.semaphore_wait(barrier, always)

    for c in rests:
        c.wait()

    def other(g, _):
        start = pl.multiple_of(g * 8, 8)
        dens = density(start)
        for a in range(groups):
            cols[me_n, pl.ds(start, 8), a * LANES:(a + 1) * LANES] = dens[a]
        return 0

    lax.fori_loop(1, points // 8, other, 0)
    for k in range(1, n_narrow):
        pltpu.make_async_remote_copy(
            src_ref=cols.at[me_n],
            dst_ref=cols.at[me_n],
            send_sem=col_send,
            recv_sem=col_recv.at[me_n],
            device_id=dev(me_w, lax.rem(me_n + k, n_narrow)),
            device_id_type=MESH,
        ).start()

    def row_units(zz, yy):
        return pl.ds(pl.multiple_of(wide_of(zz, yy, 0) * unit, 16), pair_unit)

    def send(zz, to_z, to_y, send_sem, recv_sem):
        rows = slab.at[row_units(zz, y)]
        pltpu.make_async_remote_copy(
            src_ref=rows, dst_ref=rows, send_sem=send_sem, recv_sem=recv_sem,
            device_id=dev(wide_of(to_z, to_y, xl), me_n), device_id_type=MESH,
        ).start()

    def arrived(rows, sem):
        part = slab.at[pl.ds(0, rows)]
        pltpu.make_async_copy(part, part, sem).wait()

    def to_ys(zz):
        for i, dy in enumerate((1, 3, 2)):
            send(zz, z, shift_y(dy), y_send, y_recv.at[i])

    for src in range(NX):
        @pl.when(jnp.logical_or(me_n != 0, xl != src))
        def _():
            arrived(unit, x_recv.at[src])

    for dz in range(reach, 0, -1):
        send(z, shift_z(dz), y, z_send, z_recv.at[0, dz - 1])
        send(z, shift_z(-dz), y, z_send, z_recv.at[1, dz - 1])
    to_ys(z)
    for dz in Z_ORDER:
        for way in (0, 1):
            sign = 1 - 2 * way
            arrived(pair_unit, z_recv.at[way, dz - 1])
            if dz == reach:
                for k in range(reach - way, 0, -1):
                    send(shift_z(-sign * dz), shift_z(sign * k), y, z_send, far_recv.at[way, k - 1])
            to_ys(shift_z(-sign * dz))
    for k in range(1, reach + 1):
        for way in (0, 1):
            if k > reach - way:
                continue
            sign = 1 - 2 * way
            arrived(pair_unit, far_recv.at[way, k - 1])
            to_ys(shift_z(-sign * (reach + k)))

    def row_of(ref):
        return lambda c: jnp.broadcast_to(ref[pl.ds(c, 1), :], (8, LANES))

    energies = pick(row_of(ev), row_of(ec))
    weight = jnp.concatenate(
        [1.0 / (energies[2 * a + 1] - energies[2 * a]) for a in range(groups)], axis=1
    )[0:1]
    for k in range(1, n_narrow):
        n = lax.rem(me_n + k, n_narrow)
        pltpu.make_async_copy(cols.at[n], cols.at[n], col_recv.at[n]).wait()
    columns = jnp.concatenate([cols[n] for n in range(n_narrow)], axis=0) * weight
    left_hi = columns.astype(jnp.bfloat16)
    left_lo = (columns - left_hi.astype(jnp.float32)).astype(jnp.bfloat16)
    chi_load.wait()
    for i in range(3):
        arrived(nz * pair_unit, y_recv.at[i])

    def dot(x, t):
        return lax.dot_general(
            x, t, (((1,), (1,)), ((), ())), preferred_element_type=jnp.float32
        )

    slab_rows = out_ref.shape[1]
    step = 256
    for j in range(slab_rows // step):
        right = jnp.concatenate(
            [
                slab[pl.ds(j * step * groups + a, step, stride=groups), :]
                for a in range(groups)
            ],
            axis=1,
        )
        right_hi = right.astype(jnp.bfloat16)
        right_lo = (right - right_hi.astype(jnp.float32)).astype(jnp.bfloat16)
        at = slice(j * step, (j + 1) * step)
        out_ref[:, at] = chi[:, at] + (
            dot(left_hi, right_hi) + (dot(left_hi, right_lo) + dot(left_lo, right_hi))
        )

    @pl.when(me_n == 0)
    def _():
        arrived(n_x * unit, x_send)
    whole = cols.at[pl.ds(0, n_narrow - 1)]
    pltpu.make_async_copy(whole, whole, col_send).wait()
    arrived((4 * reach - 1) * pair_unit, z_send)
    arrived(nz * pair_unit * 3, y_send)


def shards(chi_in, val_orb, cond_orb, e_val, e_cond, pair_val, pair_cond):
    n_wide, n_narrow = lax.axis_size("wide"), lax.axis_size("narrow")
    points, bands = val_orb.shape
    g_dev, slab_rows = chi_in.shape
    pairs = pair_val.shape[1]
    groups = pairs // LANES
    nz = n_wide // (NY * NX)
    reach = nz // 4
    any_space = pl.BlockSpec(memory_space=pl.ANY)
    dma = pltpu.SemaphoreType.DMA
    return pl.pallas_call(
        functools.partial(kernel, n_wide, n_narrow, pairs, reach),
        out_shape=jax.ShapeDtypeStruct(chi_in.shape, jnp.float32),
        in_specs=[any_space] * 7,
        out_specs=pl.BlockSpec(memory_space=pltpu.VMEM),
        scratch_shapes=[
            pltpu.VMEM((1, pairs), jnp.int32),
            pltpu.VMEM((1, pairs), jnp.int32),
            pltpu.VMEM((bands // LANES, LANES), jnp.float32),
            pltpu.VMEM((bands // LANES, LANES), jnp.float32),
            pltpu.VMEM((points, bands), jnp.float32),
            pltpu.VMEM((points, bands), jnp.float32),
            pltpu.VMEM((g_dev, slab_rows), jnp.float32),
            pltpu.VMEM((8 * groups, LANES), jnp.float32),
            pltpu.VMEM((slab_rows * groups, LANES), jnp.float32),
            pltpu.VMEM((n_narrow, points, pairs), jnp.float32),
            dma((9,)),
            dma,
            dma((NX,)),
            dma,
            dma((n_narrow,)),
            dma,
            dma((2, reach)),
            dma((2, reach)),
            dma,
            dma((3,)),
        ],
        compiler_params=pltpu.CompilerParams(
            collective_id=0, has_side_effects=True, vmem_limit_bytes=60 << 20
        ),
        name="chi_slab",
    )(
        pair_val,
        pair_cond,
        e_val.reshape(bands // LANES, LANES),
        e_cond.reshape(bands // LANES, LANES),
        val_orb,
        cond_orb,
        chi_in,
    )


def solution(mesh):
    placed = (
        P("wide", "narrow"),
        P(("wide", "narrow"), None),
        P(("wide", "narrow"), None),
        P(),
        P(),
        P(),
        P(),
    )
    return jax.shard_map(
        shards, mesh=mesh, in_specs=placed, out_specs=P("wide", "narrow"), check_vma=False
    )
```

```python
import functools

import jax
import jax.numpy as jnp
from jax import lax
from jax.experimental import pallas as pl
from jax.experimental.pallas import tpu as pltpu
from jax.sharding import PartitionSpec as P

MESH = pl.DeviceIdType.MESH
LANES = 128
NY = 4
NX = 2
Z_ORDER = (1, 2, 3, 8, 4, 5, 6, 7)
UNROLL = 16
EARLY = 3


def kernel(
    n_wide, n_narrow, pairs, reach,
    pv_ref, pc_ref, ev_ref, ec_ref, val_ref, cond_ref, chi_ref,
    out_ref,
    pv, pc, ev, ec, vbuf, cbuf, chi, weights, stage, slab, cols,
    permit, in_sems, x_send, x_recv, col_send, col_recv, z_send, z_recv, far_recv, y_send, y_recv,
):
    me_w = lax.axis_index("wide")
    me_n = lax.axis_index("narrow")
    nz = n_wide // (NY * NX)
    z, y, xl = me_w // (NY * NX), (me_w // NX) % NY, me_w % NX
    groups = pairs // LANES
    unit = 2 * groups
    pair_unit = unit * NX
    points = vbuf.shape[0]
    n_x = NX * n_narrow - 1

    def wide_of(zz, yy, xx):
        return (zz * NY + yy) * NX + xx

    def dev(w, n):
        return {"wide": w, "narrow": n}

    def shift_z(dz):
        return lax.rem(z + dz + nz, nz)

    def shift_y(dy):
        return lax.rem(y + dy + NY, NY)

    small = [
        pltpu.make_async_copy(s, d, in_sems.at[i])
        for i, (s, d) in enumerate([(pv_ref, pv), (pc_ref, pc), (ev_ref, ev), (ec_ref, ec)])
    ]
    heads = [
        pltpu.make_async_copy(s.at[pl.ds(0, 8)], d.at[pl.ds(0, 8)], in_sems.at[4 + i])
        for i, (s, d) in enumerate([(val_ref, vbuf), (cond_ref, cbuf)])
    ]
    rests = [
        pltpu.make_async_copy(
            s.at[pl.ds(8, points - 8)], d.at[pl.ds(8, points - 8)], in_sems.at[6 + i]
        )
        for i, (s, d) in enumerate([(val_ref, vbuf), (cond_ref, cbuf)])
    ]
    chi_load = pltpu.make_async_copy(chi_ref, chi, in_sems.at[8])
    for c in small + heads + rests + [chi_load]:
        c.start()

    barrier = pltpu.get_barrier_semaphore()

    def greet(w, n):
        pl.semaphore_signal(barrier, inc=1, device_id=dev(w, n), device_id_type=MESH)

    for src in range(NX):
        @pl.when(jnp.logical_or(me_n != 0, xl != src))
        def _():
            greet(wide_of(z, y, src), 0)
    for k in range(1, n_narrow):
        greet(me_w, lax.rem(me_n + k, n_narrow))
    for dy in (1, 3, 2):
        greet(wide_of(z, shift_y(dy), xl), me_n)
    near = reach // 2
    for dz in range(1, near + 1):
        greet(wide_of(shift_z(dz), y, xl), me_n)
        greet(wide_of(shift_z(-dz), y, xl), me_n)
    always = (n_narrow - 1) + 3 + 2 * near

    for c in small:
        c.wait()
    for c in heads:
        c.wait()

    def split(ref, a):
        index = jnp.broadcast_to(ref[0:1, a * LANES:(a + 1) * LANES], (8, LANES))
        return index & (LANES - 1), index >> 7

    idx_v = [split(pv, a) for a in range(groups)]
    idx_c = [split(pc, a) for a in range(groups)]
    chunks = vbuf.shape[1] // LANES

    def pick(load_v, load_c):
        def body(i, acc):
            for u in range(UNROLL):
                c = i * UNROLL + u
                rows_v, rows_c = load_v(c), load_c(c)
                new = []
                for a in range(groups):
                    for rows, (lo, hi), old in (
                        (rows_v, idx_v[a], acc[2 * a]),
                        (rows_c, idx_c[a], acc[2 * a + 1]),
                    ):
                        got = jnp.take_along_axis(rows, lo, axis=1, mode="promise_in_bounds")
                        new.append(jnp.where(hi == c, got, old))
                acc = tuple(new)
            return acc

        zero = jnp.zeros((8, LANES), jnp.float32)
        return lax.fori_loop(0, chunks // UNROLL, body, (zero,) * (2 * groups))

    def density(start):
        def load(ref):
            return lambda c: ref[
                pl.ds(start, 8), pl.ds(pl.multiple_of(c * LANES, LANES), LANES)
            ]

        got = pick(load(vbuf), load(cbuf))
        return [got[2 * a] * got[2 * a + 1] for a in range(groups)]

    first = density(0)
    for a in range(groups):
        stage[pl.ds(a, 8, stride=groups), :] = first[a]
        cols[me_n, pl.ds(0, 8), a * LANES:(a + 1) * LANES] = first[a]

    for c in rests:
        c.wait()

    def other(g, _):
        start = pl.multiple_of(g * 8, 8)
        dens = density(start)
        for a in range(groups):
            cols[me_n, pl.ds(start, 8), a * LANES:(a + 1) * LANES] = dens[a]
        return 0

    def row_of(ref):
        return lambda c: jnp.broadcast_to(ref[pl.ds(c, 1), :], (8, LANES))

    energies = pick(row_of(ev), row_of(ec))
    for a in range(groups):
        weights[:, a * LANES:(a + 1) * LANES] = 1.0 / (energies[2 * a + 1] - energies[2 * a])
    lax.fori_loop(1, EARLY, other, 0)

    home = wide_of(z, y, 0) * unit
    own = pl.ds(pl.multiple_of(home + xl * unit, 8), unit)

    @pl.when(me_n == 0)
    def _():
        slab[own, :] = stage[pl.ds(0, unit), :]
        pl.semaphore_wait(barrier, always + n_x)
        for k in range(1, NX * n_narrow):
            xx, n = lax.rem(xl + k // n_narrow, NX), k % n_narrow
            pltpu.make_async_remote_copy(
                src_ref=stage.at[pl.ds(n * unit, unit)],
                dst_ref=slab.at[own],
                send_sem=x_send,
                recv_sem=x_recv.at[xl],
                device_id=dev(wide_of(z, y, xx), n),
                device_id_type=MESH,
            ).start()

    @pl.when(me_n != 0)
    def _():
        pl.semaphore_wait(barrier, always)

    for way in (0, 1):
        to = shift_z((2 * way - 1) * near)
        pl.semaphore_signal(
            permit.at[way], inc=1, device_id=dev(wide_of(to, y, xl), me_n), device_id_type=MESH
        )

    lax.fori_loop(EARLY, points // 8, other, 0)
    for k in range(1, n_narrow):
        pltpu.make_async_remote_copy(
            src_ref=cols.at[me_n],
            dst_ref=cols.at[me_n],
            send_sem=col_send,
            recv_sem=col_recv.at[me_n],
            device_id=dev(me_w, lax.rem(me_n + k, n_narrow)),
            device_id_type=MESH,
        ).start()

    def row_units(zz, yy):
        return pl.ds(pl.multiple_of(wide_of(zz, yy, 0) * unit, 16), pair_unit)

    def send(zz, to_z, to_y, send_sem, recv_sem):
        rows = slab.at[row_units(zz, y)]
        pltpu.make_async_remote_copy(
            src_ref=rows, dst_ref=rows, send_sem=send_sem, recv_sem=recv_sem,
            device_id=dev(wide_of(to_z, to_y, xl), me_n), device_id_type=MESH,
        ).start()

    def arrived(rows, sem):
        part = slab.at[pl.ds(0, rows)]
        pltpu.make_async_copy(part, part, sem).wait()

    def to_ys(zz):
        for i, dy in enumerate((1, 3, 2)):
            send(zz, z, shift_y(dy), y_send, y_recv.at[i])

    for src in range(NX):
        @pl.when(jnp.logical_or(me_n != 0, xl != src))
        def _():
            arrived(unit, x_recv.at[src])

    for way in (0, 1):
        pl.semaphore_wait(permit.at[way], 1)

    for dz in range(reach, 0, -1):
        send(z, shift_z(dz), y, z_send, z_recv.at[0, dz - 1])
        send(z, shift_z(-dz), y, z_send, z_recv.at[1, dz - 1])
    to_ys(z)
    for dz in Z_ORDER:
        for way in (0, 1):
            sign = 1 - 2 * way
            arrived(pair_unit, z_recv.at[way, dz - 1])
            if dz == reach:
                for k in range(reach - way, 0, -1):
                    send(shift_z(-sign * dz), shift_z(sign * k), y, z_send, far_recv.at[way, k - 1])
            to_ys(shift_z(-sign * dz))
    for k in range(1, reach + 1):
        for way in (0, 1):
            if k > reach - way:
                continue
            sign = 1 - 2 * way
            arrived(pair_unit, far_recv.at[way, k - 1])
            to_ys(shift_z(-sign * (reach + k)))

    for k in range(1, n_narrow):
        n = lax.rem(me_n + k, n_narrow)
        pltpu.make_async_copy(cols.at[n], cols.at[n], col_recv.at[n]).wait()
    columns = jnp.concatenate([cols[n] for n in range(n_narrow)], axis=0) * weights[0:1, :]
    left_hi = columns.astype(jnp.bfloat16)
    left_lo = (columns - left_hi.astype(jnp.float32)).astype(jnp.bfloat16)
    chi_load.wait()
    for i in range(3):
        arrived(nz * pair_unit, y_recv.at[i])

    def dot(x, t):
        return lax.dot_general(
            x, t, (((1,), (1,)), ((), ())), preferred_element_type=jnp.float32
        )

    slab_rows = out_ref.shape[1]
    step = 256
    for j in range(slab_rows // step):
        right = jnp.concatenate(
            [
                slab[pl.ds(j * step * groups + a, step, stride=groups), :]
                for a in range(groups)
            ],
            axis=1,
        )
        right_hi = right.astype(jnp.bfloat16)
        right_lo = (right - right_hi.astype(jnp.float32)).astype(jnp.bfloat16)
        at = slice(j * step, (j + 1) * step)
        out_ref[:, at] = chi[:, at] + (
            dot(left_hi, right_hi) + (dot(left_hi, right_lo) + dot(left_lo, right_hi))
        )

    @pl.when(me_n == 0)
    def _():
        arrived(n_x * unit, x_send)
    whole = cols.at[pl.ds(0, n_narrow - 1)]
    pltpu.make_async_copy(whole, whole, col_send).wait()
    arrived((4 * reach - 1) * pair_unit, z_send)
    arrived(nz * pair_unit * 3, y_send)


def shards(chi_in, val_orb, cond_orb, e_val, e_cond, pair_val, pair_cond):
    n_wide, n_narrow = lax.axis_size("wide"), lax.axis_size("narrow")
    points, bands = val_orb.shape
    g_dev, slab_rows = chi_in.shape
    pairs = pair_val.shape[1]
    groups = pairs // LANES
    nz = n_wide // (NY * NX)
    reach = nz // 4
    any_space = pl.BlockSpec(memory_space=pl.ANY)
    dma = pltpu.SemaphoreType.DMA
    return pl.pallas_call(
        functools.partial(kernel, n_wide, n_narrow, pairs, reach),
        out_shape=jax.ShapeDtypeStruct(chi_in.shape, jnp.float32),
        in_specs=[any_space] * 7,
        out_specs=pl.BlockSpec(memory_space=pltpu.VMEM),
        scratch_shapes=[
            pltpu.VMEM((1, pairs), jnp.int32),
            pltpu.VMEM((1, pairs), jnp.int32),
            pltpu.VMEM((bands // LANES, LANES), jnp.float32),
            pltpu.VMEM((bands // LANES, LANES), jnp.float32),
            pltpu.VMEM((points, bands), jnp.float32),
            pltpu.VMEM((points, bands), jnp.float32),
            pltpu.VMEM((g_dev, slab_rows), jnp.float32),
            pltpu.VMEM((8, pairs), jnp.float32),
            pltpu.VMEM((8 * groups, LANES), jnp.float32),
            pltpu.VMEM((slab_rows * groups, LANES), jnp.float32),
            pltpu.VMEM((n_narrow, points, pairs), jnp.float32),
            pltpu.SemaphoreType.REGULAR((2,)),
            dma((9,)),
            dma,
            dma((NX,)),
            dma,
            dma((n_narrow,)),
            dma,
            dma((2, reach)),
            dma((2, reach)),
            dma,
            dma((3,)),
        ],
        compiler_params=pltpu.CompilerParams(
            collective_id=0, has_side_effects=True, vmem_limit_bytes=60 << 20
        ),
        name="chi_slab",
    )(
        pair_val,
        pair_cond,
        e_val.reshape(bands // LANES, LANES),
        e_cond.reshape(bands // LANES, LANES),
        val_orb,
        cond_orb,
        chi_in,
    )


def solution(mesh):
    placed = (
        P("wide", "narrow"),
        P(("wide", "narrow"), None),
        P(("wide", "narrow"), None),
        P(),
        P(),
        P(),
        P(),
    )
    return jax.shard_map(
        shards, mesh=mesh, in_specs=placed, out_specs=P("wide", "narrow"), check_vma=False
    )
```

```python
import functools

import jax
import jax.numpy as jnp
from jax import lax
from jax.experimental import pallas as pl
from jax.experimental.pallas import tpu as pltpu
from jax.sharding import PartitionSpec as P

MESH = pl.DeviceIdType.MESH
LANES = 128
NY = 4
NX = 2
TREE = {0: (8, 4, 3, 2, 1), 4: (7, 6, 5)}
RELAY = 8
ARRIVALS = (1, 2, 3, 4, 8, 5, 6, 7)
Y_SHIFTS = (2, 1, 3)
X_SHIFTS = (2, 1, 3, 0)
UNROLL = 16
EARLY = 2


def kernel(
    n_wide, n_narrow, pairs, reach,
    pv_ref, pc_ref, ev_ref, ec_ref, val_ref, cond_ref, chi_ref,
    out_ref,
    pv, pc, ev, ec, vbuf, cbuf, chi, weights, stage, slab, cols,
    permit, in_sems, x_send, x_recv, col_send, col_recv, z_send, z_recv, y_send, y_recv, pair_recv,
):
    me_w = lax.axis_index("wide")
    me_n = lax.axis_index("narrow")
    nz = n_wide // (NY * NX)
    z, y, xl = me_w // (NY * NX), (me_w // NX) % NY, me_w % NX
    groups = pairs // LANES
    unit = 2 * groups
    pair_unit = unit * NX
    points = vbuf.shape[0]
    n_x = NX * n_narrow - 1

    def wide_of(zz, yy, xx):
        return (zz * NY + yy) * NX + xx

    def dev(w, n):
        return {"wide": w, "narrow": n}

    def shift_z(dz):
        return lax.rem(z + dz + nz, nz)

    def shift_y(dy):
        return lax.rem(y + dy + NY, NY)

    small = [
        pltpu.make_async_copy(s, d, in_sems.at[i])
        for i, (s, d) in enumerate([(pv_ref, pv), (pc_ref, pc), (ev_ref, ev), (ec_ref, ec)])
    ]
    heads = [
        pltpu.make_async_copy(s.at[pl.ds(0, 8)], d.at[pl.ds(0, 8)], in_sems.at[4 + i])
        for i, (s, d) in enumerate([(val_ref, vbuf), (cond_ref, cbuf)])
    ]
    rests = [
        pltpu.make_async_copy(
            s.at[pl.ds(8, points - 8)], d.at[pl.ds(8, points - 8)], in_sems.at[6 + i]
        )
        for i, (s, d) in enumerate([(val_ref, vbuf), (cond_ref, cbuf)])
    ]
    chi_load = pltpu.make_async_copy(chi_ref, chi, in_sems.at[8])
    for c in small + heads + rests + [chi_load]:
        c.start()

    barrier = pltpu.get_barrier_semaphore()

    def greet(w, n):
        pl.semaphore_signal(barrier, inc=1, device_id=dev(w, n), device_id_type=MESH)

    for src in range(NX):
        @pl.when(jnp.logical_or(me_n != 0, xl != src))
        def _():
            greet(wide_of(z, y, src), 0)
    for k in range(1, n_narrow):
        greet(me_w, lax.rem(me_n + k, n_narrow))
    for dy in Y_SHIFTS:
        greet(wide_of(z, shift_y(dy), xl), me_n)
    for dy in X_SHIFTS:
        greet(wide_of(z, shift_y(dy), 1 - xl), me_n)
    near = reach // 2
    for dz in range(1, near + 1):
        greet(wide_of(shift_z(dz), y, xl), me_n)
        greet(wide_of(shift_z(-dz), y, xl), me_n)
    always = (n_narrow - 1) + len(Y_SHIFTS) + len(X_SHIFTS) + 2 * near

    for c in small:
        c.wait()
    for c in heads:
        c.wait()

    def split(ref, a):
        index = jnp.broadcast_to(ref[0:1, a * LANES:(a + 1) * LANES], (8, LANES))
        return index & (LANES - 1), index >> 7

    idx_v = [split(pv, a) for a in range(groups)]
    idx_c = [split(pc, a) for a in range(groups)]
    chunks = vbuf.shape[1] // LANES

    def pick(load_v, load_c):
        def body(i, acc):
            for u in range(UNROLL):
                c = i * UNROLL + u
                rows_v, rows_c = load_v(c), load_c(c)
                new = []
                for a in range(groups):
                    for rows, (lo, hi), old in (
                        (rows_v, idx_v[a], acc[2 * a]),
                        (rows_c, idx_c[a], acc[2 * a + 1]),
                    ):
                        got = jnp.take_along_axis(rows, lo, axis=1, mode="promise_in_bounds")
                        new.append(jnp.where(hi == c, got, old))
                acc = tuple(new)
            return acc

        zero = jnp.zeros((8, LANES), jnp.float32)
        return lax.fori_loop(0, chunks // UNROLL, body, (zero,) * (2 * groups))

    def density(start):
        def load(ref):
            return lambda c: ref[
                pl.ds(start, 8), pl.ds(pl.multiple_of(c * LANES, LANES), LANES)
            ]

        got = pick(load(vbuf), load(cbuf))
        return [got[2 * a] * got[2 * a + 1] for a in range(groups)]

    first = density(0)
    for a in range(groups):
        stage[pl.ds(a, 8, stride=groups), :] = first[a]
        cols[me_n, pl.ds(0, 8), a * LANES:(a + 1) * LANES] = first[a]

    for c in rests:
        c.wait()

    def other(g, _):
        start = pl.multiple_of(g * 8, 8)
        dens = density(start)
        for a in range(groups):
            cols[me_n, pl.ds(start, 8), a * LANES:(a + 1) * LANES] = dens[a]
        return 0

    lax.fori_loop(1, EARLY, other, 0)

    home = wide_of(z, y, 0) * unit
    own = pl.ds(pl.multiple_of(home + xl * unit, 8), unit)

    @pl.when(me_n == 0)
    def _():
        slab[own, :] = stage[pl.ds(0, unit), :]
        pl.semaphore_wait(barrier, always + n_x)
        for k in range(1, NX * n_narrow):
            xx, n = lax.rem(xl + k // n_narrow, NX), k % n_narrow
            pltpu.make_async_remote_copy(
                src_ref=stage.at[pl.ds(n * unit, unit)],
                dst_ref=slab.at[own],
                send_sem=x_send,
                recv_sem=x_recv.at[xl],
                device_id=dev(wide_of(z, y, xx), n),
                device_id_type=MESH,
            ).start()

    @pl.when(me_n != 0)
    def _():
        pl.semaphore_wait(barrier, always)

    for way in (0, 1):
        to = shift_z((2 * way - 1) * near)
        pl.semaphore_signal(
            permit.at[way], inc=1, device_id=dev(wide_of(to, y, xl), me_n), device_id_type=MESH
        )

    lax.fori_loop(EARLY, points // 8, other, 0)
    for k in range(1, n_narrow):
        pltpu.make_async_remote_copy(
            src_ref=cols.at[me_n],
            dst_ref=cols.at[me_n],
            send_sem=col_send,
            recv_sem=col_recv.at[me_n],
            device_id=dev(me_w, lax.rem(me_n + k, n_narrow)),
            device_id_type=MESH,
        ).start()

    def row_units(zz, yy):
        return pl.ds(pl.multiple_of(wide_of(zz, yy, 0) * unit, 16), pair_unit)

    def send(zz, to_z, to_y, to_x, send_sem, recv_sem):
        rows = slab.at[row_units(zz, y)]
        pltpu.make_async_remote_copy(
            src_ref=rows, dst_ref=rows, send_sem=send_sem, recv_sem=recv_sem,
            device_id=dev(wide_of(to_z, to_y, to_x), me_n), device_id_type=MESH,
        ).start()

    def arrived(rows, sem):
        part = slab.at[pl.ds(0, rows)]
        pltpu.make_async_copy(part, part, sem).wait()

    def to_ys(zz):
        for i, dy in enumerate(Y_SHIFTS):
            send(zz, z, shift_y(dy), xl, y_send, y_recv.at[i])

    def to_xs(zz):
        for i, dy in enumerate(X_SHIFTS):
            send(zz, z, shift_y(dy), 1 - xl, y_send, pair_recv.at[i])

    def far_loop(do):
        for i in range(reach // NX):
            at = reach + 1 + NX * i + xl
            do(0, at)
            if i < reach // NX - 1:
                do(1, at)
            else:
                pl.when(xl == 0)(functools.partial(do, 1, at))

    for src in range(NX):
        @pl.when(jnp.logical_or(me_n != 0, xl != src))
        def _():
            arrived(unit, x_recv.at[src])

    for way in (0, 1):
        pl.semaphore_wait(permit.at[way], 1)

    def z_sends(way, at):
        sign = 1 - 2 * way
        for to in TREE[at]:
            send(
                shift_z(-sign * at), shift_z(sign * (to - at)), y, xl,
                z_send, z_recv.at[way, to - 1],
            )

    def relay(way, to):
        sign = 1 - 2 * way
        send(
            shift_z(-sign * RELAY), shift_z(sign * (to - RELAY)), y, xl,
            z_send, z_recv.at[way, to - 1],
        )

    def far_arrive(way, at):
        arrived(pair_unit, z_recv.at[way, at - 1])
        zz = shift_z((2 * way - 1) * at)
        to_xs(zz)
        to_ys(zz)

    for way in (0, 1):
        z_sends(way, 0)
    to_ys(z)
    def row_of(ref):
        return lambda c: jnp.broadcast_to(ref[pl.ds(c, 1), :], (8, LANES))

    energies = pick(row_of(ev), row_of(ec))
    for a in range(groups):
        weights[:, a * LANES:(a + 1) * LANES] = 1.0 / (energies[2 * a + 1] - energies[2 * a])
    for at in ARRIVALS:
        for way in (0, 1):
            arrived(pair_unit, z_recv.at[way, at - 1])
            if at in TREE:
                z_sends(way, at)
        if at == RELAY:
            far_loop(relay)
        for way in (0, 1):
            to_ys(shift_z((2 * way - 1) * at))
    far_loop(far_arrive)

    for k in range(1, n_narrow):
        n = lax.rem(me_n + k, n_narrow)
        pltpu.make_async_copy(cols.at[n], cols.at[n], col_recv.at[n]).wait()
    columns = jnp.concatenate([cols[n] for n in range(n_narrow)], axis=0) * weights[0:1, :]
    left_hi = columns.astype(jnp.bfloat16)
    left_lo = (columns - left_hi.astype(jnp.float32)).astype(jnp.bfloat16)
    chi_load.wait()
    n_near = 1 + 2 * reach
    n_far = (reach, reach - 1)
    for c in range(NX):
        @pl.when(xl == c)
        def _():
            for i in range(len(Y_SHIFTS)):
                arrived((n_near + n_far[c]) * pair_unit, y_recv.at[i])
            for i in range(len(X_SHIFTS)):
                arrived(n_far[1 - c] * pair_unit, pair_recv.at[i])


    def dot(x, t):
        return lax.dot_general(
            x, t, (((1,), (1,)), ((), ())), preferred_element_type=jnp.float32
        )

    slab_rows = out_ref.shape[1]
    step = 256
    for j in range(slab_rows // step):
        right = jnp.concatenate(
            [
                slab[pl.ds(j * step * groups + a, step, stride=groups), :]
                for a in range(groups)
            ],
            axis=1,
        )
        right_hi = right.astype(jnp.bfloat16)
        right_lo = (right - right_hi.astype(jnp.float32)).astype(jnp.bfloat16)
        at = slice(j * step, (j + 1) * step)
        out_ref[:, at] = chi[:, at] + (
            dot(left_hi, right_hi) + (dot(left_hi, right_lo) + dot(left_lo, right_hi))
        )

    @pl.when(me_n == 0)
    def _():
        arrived(n_x * unit, x_send)
    whole = cols.at[pl.ds(0, n_narrow - 1)]
    pltpu.make_async_copy(whole, whole, col_send).wait()
    for c in range(NX):
        @pl.when(xl == c)
        def _():
            n_y, n_x_shifts = len(Y_SHIFTS), len(X_SHIFTS)
            arrived((n_near - 1 + n_far[c]) * pair_unit, z_send)
            arrived((n_y * n_near + (n_y + n_x_shifts) * n_far[c]) * pair_unit, y_send)


def shards(chi_in, val_orb, cond_orb, e_val, e_cond, pair_val, pair_cond):
    n_wide, n_narrow = lax.axis_size("wide"), lax.axis_size("narrow")
    points, bands = val_orb.shape
    g_dev, slab_rows = chi_in.shape
    pairs = pair_val.shape[1]
    groups = pairs // LANES
    nz = n_wide // (NY * NX)
    reach = nz // 4
    any_space = pl.BlockSpec(memory_space=pl.ANY)
    dma = pltpu.SemaphoreType.DMA
    return pl.pallas_call(
        functools.partial(kernel, n_wide, n_narrow, pairs, reach),
        out_shape=jax.ShapeDtypeStruct(chi_in.shape, jnp.float32),
        in_specs=[any_space] * 7,
        out_specs=pl.BlockSpec(memory_space=pltpu.VMEM),
        scratch_shapes=[
            pltpu.VMEM((1, pairs), jnp.int32),
            pltpu.VMEM((1, pairs), jnp.int32),
            pltpu.VMEM((bands // LANES, LANES), jnp.float32),
            pltpu.VMEM((bands // LANES, LANES), jnp.float32),
            pltpu.VMEM((points, bands), jnp.float32),
            pltpu.VMEM((points, bands), jnp.float32),
            pltpu.VMEM((g_dev, slab_rows), jnp.float32),
            pltpu.VMEM((8, pairs), jnp.float32),
            pltpu.VMEM((8 * groups, LANES), jnp.float32),
            pltpu.VMEM((slab_rows * groups, LANES), jnp.float32),
            pltpu.VMEM((n_narrow, points, pairs), jnp.float32),
            pltpu.SemaphoreType.REGULAR((2,)),
            dma((9,)),
            dma,
            dma((NX,)),
            dma,
            dma((n_narrow,)),
            dma,
            dma((2, 2 * reach)),
            dma,
            dma((len(Y_SHIFTS),)),
            dma((len(X_SHIFTS),)),
        ],
        compiler_params=pltpu.CompilerParams(
            collective_id=0, has_side_effects=True, vmem_limit_bytes=60 << 20
        ),
        name="chi_slab",
    )(
        pair_val,
        pair_cond,
        e_val.reshape(bands // LANES, LANES),
        e_cond.reshape(bands // LANES, LANES),
        val_orb,
        cond_orb,
        chi_in,
    )


def solution(mesh):
    placed = (
        P("wide", "narrow"),
        P(("wide", "narrow"), None),
        P(("wide", "narrow"), None),
        P(),
        P(),
        P(),
        P(),
    )
    return jax.shard_map(
        shards, mesh=mesh, in_specs=placed, out_specs=P("wide", "narrow"), check_vma=False
    )
```

```python
import functools

import jax
import jax.numpy as jnp
from jax import lax
from jax.experimental import pallas as pl
from jax.experimental.pallas import tpu as pltpu
from jax.sharding import PartitionSpec as P

MESH = pl.DeviceIdType.MESH
LANES = 128
NY = 4
NX = 2
TREE = {0: (8, 4, 3, 2, 1), 4: (7, 6, 5)}
RELAY = 8
ARRIVALS = (1, 2, 3, 4, 8, 5, 6, 7)
Y_SHIFTS = (2, 1, 3)
X_SHIFTS = (2, 1, 3, 0)
UNROLL = 16
EARLY = 2


def kernel(
    n_wide, n_narrow, pairs, reach,
    pv_ref, pc_ref, ev_ref, ec_ref, val_ref, cond_ref, chi_ref,
    out_ref,
    pv, pc, ev, ec, vbuf, cbuf, chi, weights, stage, slab, cols,
    permit, in_sems, x_send, x_recv, col_send, col_recv, z_send, z_recv, y_send, y_recv, pair_recv,
):
    me_w = lax.axis_index("wide")
    me_n = lax.axis_index("narrow")
    nz = n_wide // (NY * NX)
    z, y, xl = me_w // (NY * NX), (me_w // NX) % NY, me_w % NX
    groups = pairs // LANES
    unit = 2 * groups
    pair_unit = unit * NX
    points = vbuf.shape[0]
    n_x = NX * n_narrow - 1

    def wide_of(zz, yy, xx):
        return (zz * NY + yy) * NX + xx

    def dev(w, n):
        return {"wide": w, "narrow": n}

    def shift_z(dz):
        return lax.rem(z + dz + nz, nz)

    def shift_y(dy):
        return lax.rem(y + dy + NY, NY)

    small = [
        pltpu.make_async_copy(s, d, in_sems.at[i])
        for i, (s, d) in enumerate([(pv_ref, pv), (pc_ref, pc), (ev_ref, ev), (ec_ref, ec)])
    ]
    heads = [
        pltpu.make_async_copy(s.at[pl.ds(0, 8)], d.at[pl.ds(0, 8)], in_sems.at[4 + i])
        for i, (s, d) in enumerate([(val_ref, vbuf), (cond_ref, cbuf)])
    ]
    rests = [
        pltpu.make_async_copy(
            s.at[pl.ds(8, points - 8)], d.at[pl.ds(8, points - 8)], in_sems.at[6 + i]
        )
        for i, (s, d) in enumerate([(val_ref, vbuf), (cond_ref, cbuf)])
    ]
    chi_load = pltpu.make_async_copy(chi_ref, chi, in_sems.at[8])
    for c in heads + small + rests + [chi_load]:
        c.start()

    barrier = pltpu.get_barrier_semaphore()

    def greet(w, n):
        pl.semaphore_signal(barrier, inc=1, device_id=dev(w, n), device_id_type=MESH)

    near = reach // 2
    for dz in range(near, 0, -1):
        greet(wide_of(shift_z(dz), y, xl), me_n)
        greet(wide_of(shift_z(-dz), y, xl), me_n)
    for src in range(NX):
        @pl.when(jnp.logical_or(me_n != 0, xl != src))
        def _():
            greet(wide_of(z, y, src), 0)
    for k in range(1, n_narrow):
        greet(me_w, lax.rem(me_n + k, n_narrow))
    for dy in Y_SHIFTS:
        greet(wide_of(z, shift_y(dy), xl), me_n)
    for dy in X_SHIFTS:
        greet(wide_of(z, shift_y(dy), 1 - xl), me_n)
    always = (n_narrow - 1) + len(Y_SHIFTS) + len(X_SHIFTS) + 2 * near

    for c in small:
        c.wait()
    for c in heads:
        c.wait()

    def split(ref, a):
        index = jnp.broadcast_to(ref[0:1, a * LANES:(a + 1) * LANES], (8, LANES))
        return index & (LANES - 1), index >> 7

    idx_v = [split(pv, a) for a in range(groups)]
    idx_c = [split(pc, a) for a in range(groups)]
    chunks = vbuf.shape[1] // LANES

    def pick(load_v, load_c):
        def body(i, acc):
            for u in range(UNROLL):
                c = i * UNROLL + u
                rows_v, rows_c = load_v(c), load_c(c)
                new = []
                for a in range(groups):
                    for rows, (lo, hi), old in (
                        (rows_v, idx_v[a], acc[2 * a]),
                        (rows_c, idx_c[a], acc[2 * a + 1]),
                    ):
                        got = jnp.take_along_axis(rows, lo, axis=1, mode="promise_in_bounds")
                        new.append(jnp.where(hi == c, got, old))
                acc = tuple(new)
            return acc

        zero = jnp.zeros((8, LANES), jnp.float32)
        return lax.fori_loop(0, chunks // UNROLL, body, (zero,) * (2 * groups))

    def density(start):
        def load(ref):
            return lambda c: ref[
                pl.ds(start, 8), pl.ds(pl.multiple_of(c * LANES, LANES), LANES)
            ]

        got = pick(load(vbuf), load(cbuf))
        return [got[2 * a] * got[2 * a + 1] for a in range(groups)]

    first = density(0)
    for a in range(groups):
        stage[pl.ds(a, 8, stride=groups), :] = first[a]
        cols[me_n, pl.ds(0, 8), a * LANES:(a + 1) * LANES] = first[a]

    for c in rests:
        c.wait()

    def other(g, _):
        start = pl.multiple_of(g * 8, 8)
        dens = density(start)
        for a in range(groups):
            cols[me_n, pl.ds(start, 8), a * LANES:(a + 1) * LANES] = dens[a]
        return 0

    lax.fori_loop(1, EARLY, other, 0)

    home = wide_of(z, y, 0) * unit
    own = pl.ds(pl.multiple_of(home + xl * unit, 8), unit)

    @pl.when(me_n == 0)
    def _():
        slab[own, :] = stage[pl.ds(0, unit), :]
        pl.semaphore_wait(barrier, always + n_x)
        for k in range(1, NX * n_narrow):
            xx, n = lax.rem(xl + k // n_narrow, NX), k % n_narrow
            pltpu.make_async_remote_copy(
                src_ref=stage.at[pl.ds(n * unit, unit)],
                dst_ref=slab.at[own],
                send_sem=x_send,
                recv_sem=x_recv.at[xl],
                device_id=dev(wide_of(z, y, xx), n),
                device_id_type=MESH,
            ).start()

    @pl.when(me_n != 0)
    def _():
        pl.semaphore_wait(barrier, always)

    for way in (0, 1):
        to = shift_z((2 * way - 1) * near)
        pl.semaphore_signal(
            permit.at[way], inc=1, device_id=dev(wide_of(to, y, xl), me_n), device_id_type=MESH
        )

    lax.fori_loop(EARLY, points // 8, other, 0)
    for k in range(1, n_narrow):
        pltpu.make_async_remote_copy(
            src_ref=cols.at[me_n],
            dst_ref=cols.at[me_n],
            send_sem=col_send,
            recv_sem=col_recv.at[me_n],
            device_id=dev(me_w, lax.rem(me_n + k, n_narrow)),
            device_id_type=MESH,
        ).start()

    def row_units(zz, yy):
        return pl.ds(pl.multiple_of(wide_of(zz, yy, 0) * unit, 16), pair_unit)

    def send(zz, to_z, to_y, to_x, send_sem, recv_sem):
        rows = slab.at[row_units(zz, y)]
        pltpu.make_async_remote_copy(
            src_ref=rows, dst_ref=rows, send_sem=send_sem, recv_sem=recv_sem,
            device_id=dev(wide_of(to_z, to_y, to_x), me_n), device_id_type=MESH,
        ).start()

    def arrived(rows, sem):
        part = slab.at[pl.ds(0, rows)]
        pltpu.make_async_copy(part, part, sem).wait()

    def to_ys(zz):
        for i, dy in enumerate(Y_SHIFTS):
            send(zz, z, shift_y(dy), xl, y_send, y_recv.at[i])

    def to_xs(zz):
        for i, dy in enumerate(X_SHIFTS):
            send(zz, z, shift_y(dy), 1 - xl, y_send, pair_recv.at[i])

    def far_loop(do, order):
        for i in order(range(reach // NX)):
            at = reach + 1 + NX * i + xl
            do(0, at)
            if i < reach // NX - 1:
                do(1, at)
            else:
                pl.when(xl == 0)(functools.partial(do, 1, at))

    for src in range(NX):
        @pl.when(jnp.logical_or(me_n != 0, xl != src))
        def _():
            arrived(unit, x_recv.at[src])

    for way in (0, 1):
        pl.semaphore_wait(permit.at[way], 1)

    def z_sends(way, at):
        sign = 1 - 2 * way
        for to in TREE[at]:
            send(
                shift_z(-sign * at), shift_z(sign * (to - at)), y, xl,
                z_send, z_recv.at[way, to - 1],
            )

    def relay(way, to):
        sign = 1 - 2 * way
        send(
            shift_z(-sign * RELAY), shift_z(sign * (to - RELAY)), y, xl,
            z_send, z_recv.at[way, to - 1],
        )

    def far_arrive(way, at):
        arrived(pair_unit, z_recv.at[way, at - 1])
        zz = shift_z((2 * way - 1) * at)
        to_xs(zz)
        to_ys(zz)

    for way in (0, 1):
        z_sends(way, 0)
    to_ys(z)
    def row_of(ref):
        return lambda c: jnp.broadcast_to(ref[pl.ds(c, 1), :], (8, LANES))

    energies = pick(row_of(ev), row_of(ec))
    for a in range(groups):
        weights[:, a * LANES:(a + 1) * LANES] = 1.0 / (energies[2 * a + 1] - energies[2 * a])
    for at in ARRIVALS:
        for way in (0, 1):
            arrived(pair_unit, z_recv.at[way, at - 1])
            if at in TREE:
                z_sends(way, at)
        if at == RELAY:
            far_loop(relay, reversed)
        for way in (0, 1):
            to_ys(shift_z((2 * way - 1) * at))
    far_loop(far_arrive, iter)

    for k in range(1, n_narrow):
        n = lax.rem(me_n + k, n_narrow)
        pltpu.make_async_copy(cols.at[n], cols.at[n], col_recv.at[n]).wait()
    columns = jnp.concatenate([cols[n] for n in range(n_narrow)], axis=0) * weights[0:1, :]
    left_hi = columns.astype(jnp.bfloat16)
    left_lo = (columns - left_hi.astype(jnp.float32)).astype(jnp.bfloat16)
    chi_load.wait()
    n_near = 1 + 2 * reach
    n_far = (reach, reach - 1)
    for c in range(NX):
        @pl.when(xl == c)
        def _():
            for i in range(len(Y_SHIFTS)):
                arrived((n_near + n_far[c]) * pair_unit, y_recv.at[i])
            for i in range(len(X_SHIFTS)):
                arrived(n_far[1 - c] * pair_unit, pair_recv.at[i])


    def dot(x, t):
        return lax.dot_general(
            x, t, (((1,), (1,)), ((), ())), preferred_element_type=jnp.float32
        )

    slab_rows = out_ref.shape[1]
    step = 256
    for j in range(slab_rows // step):
        right = jnp.concatenate(
            [
                slab[pl.ds(j * step * groups + a, step, stride=groups), :]
                for a in range(groups)
            ],
            axis=1,
        )
        right_hi = right.astype(jnp.bfloat16)
        right_lo = (right - right_hi.astype(jnp.float32)).astype(jnp.bfloat16)
        at = slice(j * step, (j + 1) * step)
        out_ref[:, at] = chi[:, at] + (
            dot(left_hi, right_hi) + (dot(left_hi, right_lo) + dot(left_lo, right_hi))
        )

    @pl.when(me_n == 0)
    def _():
        arrived(n_x * unit, x_send)
    whole = cols.at[pl.ds(0, n_narrow - 1)]
    pltpu.make_async_copy(whole, whole, col_send).wait()
    for c in range(NX):
        @pl.when(xl == c)
        def _():
            n_y, n_x_shifts = len(Y_SHIFTS), len(X_SHIFTS)
            arrived((n_near - 1 + n_far[c]) * pair_unit, z_send)
            arrived((n_y * n_near + (n_y + n_x_shifts) * n_far[c]) * pair_unit, y_send)


def shards(chi_in, val_orb, cond_orb, e_val, e_cond, pair_val, pair_cond):
    n_wide, n_narrow = lax.axis_size("wide"), lax.axis_size("narrow")
    points, bands = val_orb.shape
    g_dev, slab_rows = chi_in.shape
    pairs = pair_val.shape[1]
    groups = pairs // LANES
    nz = n_wide // (NY * NX)
    reach = nz // 4
    any_space = pl.BlockSpec(memory_space=pl.ANY)
    dma = pltpu.SemaphoreType.DMA
    return pl.pallas_call(
        functools.partial(kernel, n_wide, n_narrow, pairs, reach),
        out_shape=jax.ShapeDtypeStruct(chi_in.shape, jnp.float32),
        in_specs=[any_space] * 7,
        out_specs=pl.BlockSpec(memory_space=pltpu.VMEM),
        scratch_shapes=[
            pltpu.VMEM((1, pairs), jnp.int32),
            pltpu.VMEM((1, pairs), jnp.int32),
            pltpu.VMEM((bands // LANES, LANES), jnp.float32),
            pltpu.VMEM((bands // LANES, LANES), jnp.float32),
            pltpu.VMEM((points, bands), jnp.float32),
            pltpu.VMEM((points, bands), jnp.float32),
            pltpu.VMEM((g_dev, slab_rows), jnp.float32),
            pltpu.VMEM((8, pairs), jnp.float32),
            pltpu.VMEM((8 * groups, LANES), jnp.float32),
            pltpu.VMEM((slab_rows * groups, LANES), jnp.float32),
            pltpu.VMEM((n_narrow, points, pairs), jnp.float32),
            pltpu.SemaphoreType.REGULAR((2,)),
            dma((9,)),
            dma,
            dma((NX,)),
            dma,
            dma((n_narrow,)),
            dma,
            dma((2, 2 * reach)),
            dma,
            dma((len(Y_SHIFTS),)),
            dma((len(X_SHIFTS),)),
        ],
        compiler_params=pltpu.CompilerParams(
            collective_id=0, has_side_effects=True, vmem_limit_bytes=60 << 20
        ),
        name="chi_slab",
    )(
        pair_val,
        pair_cond,
        e_val.reshape(bands // LANES, LANES),
        e_cond.reshape(bands // LANES, LANES),
        val_orb,
        cond_orb,
        chi_in,
    )


def solution(mesh):
    placed = (
        P("wide", "narrow"),
        P(("wide", "narrow"), None),
        P(("wide", "narrow"), None),
        P(),
        P(),
        P(),
        P(),
    )
    return jax.shard_map(
        shards, mesh=mesh, in_specs=placed, out_specs=P("wide", "narrow"), check_vma=False
    )
```

```python
import functools

import jax
import jax.numpy as jnp
from jax import lax
from jax.experimental import pallas as pl
from jax.experimental.pallas import tpu as pltpu
from jax.sharding import PartitionSpec as P

MESH = pl.DeviceIdType.MESH
LANES = 128
NY = 4
NX = 2
TREE = {0: (8, 4, 2, 1), 2: (3,), 4: (6, 5), 6: (7,)}
RELAY = 8
ARRIVALS = (1, 2, 4, 3, 8, 5, 6, 7)
Y_SHIFTS = (2, 1, 3)
X_SHIFTS = (2, 1, 3, 0)
UNROLL = 16
EARLY = 2


def kernel(
    n_wide, n_narrow, pairs, reach,
    pv_ref, pc_ref, ev_ref, ec_ref, val_ref, cond_ref, chi_ref,
    out_ref,
    pv, pc, ev, ec, vbuf, cbuf, chi, weights, stage, slab, cols,
    permit, in_sems, x_send, x_recv, col_send, col_recv, z_send, z_recv, y_send, y_recv, pair_recv,
):
    me_w = lax.axis_index("wide")
    me_n = lax.axis_index("narrow")
    nz = n_wide // (NY * NX)
    z, y, xl = me_w // (NY * NX), (me_w // NX) % NY, me_w % NX
    groups = pairs // LANES
    unit = 2 * groups
    pair_unit = unit * NX
    points = vbuf.shape[0]
    n_x = NX * n_narrow - 1

    def wide_of(zz, yy, xx):
        return (zz * NY + yy) * NX + xx

    def dev(w, n):
        return {"wide": w, "narrow": n}

    def shift_z(dz):
        return lax.rem(z + dz + nz, nz)

    def shift_y(dy):
        return lax.rem(y + dy + NY, NY)

    small = [
        pltpu.make_async_copy(s, d, in_sems.at[i])
        for i, (s, d) in enumerate([(pv_ref, pv), (pc_ref, pc), (ev_ref, ev), (ec_ref, ec)])
    ]
    heads = [
        pltpu.make_async_copy(s.at[pl.ds(0, 8)], d.at[pl.ds(0, 8)], in_sems.at[4 + i])
        for i, (s, d) in enumerate([(val_ref, vbuf), (cond_ref, cbuf)])
    ]
    rests = [
        pltpu.make_async_copy(
            s.at[pl.ds(8, points - 8)], d.at[pl.ds(8, points - 8)], in_sems.at[6 + i]
        )
        for i, (s, d) in enumerate([(val_ref, vbuf), (cond_ref, cbuf)])
    ]
    chi_load = pltpu.make_async_copy(chi_ref, chi, in_sems.at[8])
    for c in heads + small + rests + [chi_load]:
        c.start()

    barrier = pltpu.get_barrier_semaphore()

    def greet(w, n):
        pl.semaphore_signal(barrier, inc=1, device_id=dev(w, n), device_id_type=MESH)

    near = reach // 2
    for dz in range(near, 0, -1):
        greet(wide_of(shift_z(dz), y, xl), me_n)
        greet(wide_of(shift_z(-dz), y, xl), me_n)
    for src in range(NX):
        @pl.when(jnp.logical_or(me_n != 0, xl != src))
        def _():
            greet(wide_of(z, y, src), 0)
    for k in range(1, n_narrow):
        greet(me_w, lax.rem(me_n + k, n_narrow))
    for dy in Y_SHIFTS:
        greet(wide_of(z, shift_y(dy), xl), me_n)
    for dy in X_SHIFTS:
        greet(wide_of(z, shift_y(dy), 1 - xl), me_n)
    always = (n_narrow - 1) + len(Y_SHIFTS) + len(X_SHIFTS) + 2 * near

    for c in small:
        c.wait()
    for c in heads:
        c.wait()

    def split(ref, a):
        index = jnp.broadcast_to(ref[0:1, a * LANES:(a + 1) * LANES], (8, LANES))
        return index & (LANES - 1), index >> 7

    idx_v = [split(pv, a) for a in range(groups)]
    idx_c = [split(pc, a) for a in range(groups)]
    chunks = vbuf.shape[1] // LANES

    def pick(load_v, load_c):
        def body(i, acc):
            for u in range(UNROLL):
                c = i * UNROLL + u
                rows_v, rows_c = load_v(c), load_c(c)
                new = []
                for a in range(groups):
                    for rows, (lo, hi), old in (
                        (rows_v, idx_v[a], acc[2 * a]),
                        (rows_c, idx_c[a], acc[2 * a + 1]),
                    ):
                        got = jnp.take_along_axis(rows, lo, axis=1, mode="promise_in_bounds")
                        new.append(jnp.where(hi == c, got, old))
                acc = tuple(new)
            return acc

        zero = jnp.zeros((8, LANES), jnp.float32)
        return lax.fori_loop(0, chunks // UNROLL, body, (zero,) * (2 * groups))

    def density(start):
        def load(ref):
            return lambda c: ref[
                pl.ds(start, 8), pl.ds(pl.multiple_of(c * LANES, LANES), LANES)
            ]

        got = pick(load(vbuf), load(cbuf))
        return [got[2 * a] * got[2 * a + 1] for a in range(groups)]

    first = density(0)
    for a in range(groups):
        stage[pl.ds(a, 8, stride=groups), :] = first[a]
        cols[me_n, pl.ds(0, 8), a * LANES:(a + 1) * LANES] = first[a]

    for c in rests:
        c.wait()

    def other(g, _):
        start = pl.multiple_of(g * 8, 8)
        dens = density(start)
        for a in range(groups):
            cols[me_n, pl.ds(start, 8), a * LANES:(a + 1) * LANES] = dens[a]
        return 0

    lax.fori_loop(1, EARLY, other, 0)

    home = wide_of(z, y, 0) * unit
    own = pl.ds(pl.multiple_of(home + xl * unit, 8), unit)

    @pl.when(me_n == 0)
    def _():
        slab[own, :] = stage[pl.ds(0, unit), :]
        pl.semaphore_wait(barrier, always + n_x)
        for k in range(1, NX * n_narrow):
            xx, n = lax.rem(xl + k // n_narrow, NX), k % n_narrow
            pltpu.make_async_remote_copy(
                src_ref=stage.at[pl.ds(n * unit, unit)],
                dst_ref=slab.at[own],
                send_sem=x_send,
                recv_sem=x_recv.at[xl],
                device_id=dev(wide_of(z, y, xx), n),
                device_id_type=MESH,
            ).start()

    @pl.when(me_n != 0)
    def _():
        pl.semaphore_wait(barrier, always)

    for way in (0, 1):
        to = shift_z((2 * way - 1) * near)
        pl.semaphore_signal(
            permit.at[way], inc=1, device_id=dev(wide_of(to, y, xl), me_n), device_id_type=MESH
        )

    lax.fori_loop(EARLY, points // 8, other, 0)
    for k in range(1, n_narrow):
        pltpu.make_async_remote_copy(
            src_ref=cols.at[me_n],
            dst_ref=cols.at[me_n],
            send_sem=col_send,
            recv_sem=col_recv.at[me_n],
            device_id=dev(me_w, lax.rem(me_n + k, n_narrow)),
            device_id_type=MESH,
        ).start()

    def row_units(zz, yy):
        return pl.ds(pl.multiple_of(wide_of(zz, yy, 0) * unit, 16), pair_unit)

    def send(zz, to_z, to_y, to_x, send_sem, recv_sem):
        rows = slab.at[row_units(zz, y)]
        pltpu.make_async_remote_copy(
            src_ref=rows, dst_ref=rows, send_sem=send_sem, recv_sem=recv_sem,
            device_id=dev(wide_of(to_z, to_y, to_x), me_n), device_id_type=MESH,
        ).start()

    def arrived(rows, sem):
        part = slab.at[pl.ds(0, rows)]
        pltpu.make_async_copy(part, part, sem).wait()

    def to_ys(zz):
        for i, dy in enumerate(Y_SHIFTS):
            send(zz, z, shift_y(dy), xl, y_send, y_recv.at[i])

    def to_xs(zz):
        for i, dy in enumerate(X_SHIFTS):
            send(zz, z, shift_y(dy), 1 - xl, y_send, pair_recv.at[i])

    def far_loop(do, order):
        for i in order(range(reach // NX)):
            at = reach + 1 + NX * i + xl
            do(0, at)
            if i < reach // NX - 1:
                do(1, at)
            else:
                pl.when(xl == 0)(functools.partial(do, 1, at))

    for src in range(NX):
        @pl.when(jnp.logical_or(me_n != 0, xl != src))
        def _():
            arrived(unit, x_recv.at[src])

    for way in (0, 1):
        pl.semaphore_wait(permit.at[way], 1)

    def z_sends(way, at):
        sign = 1 - 2 * way
        for to in TREE[at]:
            send(
                shift_z(-sign * at), shift_z(sign * (to - at)), y, xl,
                z_send, z_recv.at[way, to - 1],
            )

    def relay(way, to):
        sign = 1 - 2 * way
        send(
            shift_z(-sign * RELAY), shift_z(sign * (to - RELAY)), y, xl,
            z_send, z_recv.at[way, to - 1],
        )

    def far_arrive(way, at):
        arrived(pair_unit, z_recv.at[way, at - 1])
        zz = shift_z((2 * way - 1) * at)
        to_xs(zz)
        to_ys(zz)

    for way in (0, 1):
        z_sends(way, 0)
    to_ys(z)
    def row_of(ref):
        return lambda c: jnp.broadcast_to(ref[pl.ds(c, 1), :], (8, LANES))

    energies = pick(row_of(ev), row_of(ec))
    for a in range(groups):
        weights[:, a * LANES:(a + 1) * LANES] = 1.0 / (energies[2 * a + 1] - energies[2 * a])
    for at in ARRIVALS:
        for way in (0, 1):
            arrived(pair_unit, z_recv.at[way, at - 1])
            if at in TREE:
                z_sends(way, at)
        if at == RELAY:
            far_loop(relay, reversed)
        for way in (0, 1):
            to_ys(shift_z((2 * way - 1) * at))
    far_loop(far_arrive, iter)

    for k in range(1, n_narrow):
        n = lax.rem(me_n + k, n_narrow)
        pltpu.make_async_copy(cols.at[n], cols.at[n], col_recv.at[n]).wait()
    columns = jnp.concatenate([cols[n] for n in range(n_narrow)], axis=0) * weights[0:1, :]
    left_hi = columns.astype(jnp.bfloat16)
    left_lo = (columns - left_hi.astype(jnp.float32)).astype(jnp.bfloat16)
    chi_load.wait()
    n_near = 1 + 2 * reach
    n_far = (reach, reach - 1)
    for c in range(NX):
        @pl.when(xl == c)
        def _():
            for i in range(len(Y_SHIFTS)):
                arrived((n_near + n_far[c]) * pair_unit, y_recv.at[i])
            for i in range(len(X_SHIFTS)):
                arrived(n_far[1 - c] * pair_unit, pair_recv.at[i])


    def dot(x, t):
        return lax.dot_general(
            x, t, (((1,), (1,)), ((), ())), preferred_element_type=jnp.float32
        )

    slab_rows = out_ref.shape[1]
    step = 256
    for j in range(slab_rows // step):
        right = jnp.concatenate(
            [
                slab[pl.ds(j * step * groups + a, step, stride=groups), :]
                for a in range(groups)
            ],
            axis=1,
        )
        right_hi = right.astype(jnp.bfloat16)
        right_lo = (right - right_hi.astype(jnp.float32)).astype(jnp.bfloat16)
        at = slice(j * step, (j + 1) * step)
        out_ref[:, at] = chi[:, at] + (
            dot(left_hi, right_hi) + (dot(left_hi, right_lo) + dot(left_lo, right_hi))
        )

    @pl.when(me_n == 0)
    def _():
        arrived(n_x * unit, x_send)
    whole = cols.at[pl.ds(0, n_narrow - 1)]
    pltpu.make_async_copy(whole, whole, col_send).wait()
    for c in range(NX):
        @pl.when(xl == c)
        def _():
            n_y, n_x_shifts = len(Y_SHIFTS), len(X_SHIFTS)
            arrived((n_near - 1 + n_far[c]) * pair_unit, z_send)
            arrived((n_y * n_near + (n_y + n_x_shifts) * n_far[c]) * pair_unit, y_send)


def shards(chi_in, val_orb, cond_orb, e_val, e_cond, pair_val, pair_cond):
    n_wide, n_narrow = lax.axis_size("wide"), lax.axis_size("narrow")
    points, bands = val_orb.shape
    g_dev, slab_rows = chi_in.shape
    pairs = pair_val.shape[1]
    groups = pairs // LANES
    nz = n_wide // (NY * NX)
    reach = nz // 4
    any_space = pl.BlockSpec(memory_space=pl.ANY)
    dma = pltpu.SemaphoreType.DMA
    return pl.pallas_call(
        functools.partial(kernel, n_wide, n_narrow, pairs, reach),
        out_shape=jax.ShapeDtypeStruct(chi_in.shape, jnp.float32),
        in_specs=[any_space] * 7,
        out_specs=pl.BlockSpec(memory_space=pltpu.VMEM),
        scratch_shapes=[
            pltpu.VMEM((1, pairs), jnp.int32),
            pltpu.VMEM((1, pairs), jnp.int32),
            pltpu.VMEM((bands // LANES, LANES), jnp.float32),
            pltpu.VMEM((bands // LANES, LANES), jnp.float32),
            pltpu.VMEM((points, bands), jnp.float32),
            pltpu.VMEM((points, bands), jnp.float32),
            pltpu.VMEM((g_dev, slab_rows), jnp.float32),
            pltpu.VMEM((8, pairs), jnp.float32),
            pltpu.VMEM((8 * groups + 8, LANES), jnp.float32),
            pltpu.VMEM((slab_rows * groups + 8, LANES), jnp.float32),
            pltpu.VMEM((n_narrow, points, pairs), jnp.float32),
            pltpu.SemaphoreType.REGULAR((2,)),
            dma((9,)),
            dma,
            dma((NX,)),
            dma,
            dma((n_narrow,)),
            dma,
            dma((2, 2 * reach)),
            dma,
            dma((len(Y_SHIFTS),)),
            dma((len(X_SHIFTS),)),
        ],
        compiler_params=pltpu.CompilerParams(
            collective_id=0, has_side_effects=True, vmem_limit_bytes=60 << 20
        ),
        name="chi_slab",
    )(
        pair_val,
        pair_cond,
        e_val.reshape(bands // LANES, LANES),
        e_cond.reshape(bands // LANES, LANES),
        val_orb,
        cond_orb,
        chi_in,
    )


def solution(mesh):
    placed = (
        P("wide", "narrow"),
        P(("wide", "narrow"), None),
        P(("wide", "narrow"), None),
        P(),
        P(),
        P(),
        P(),
    )
    return jax.shard_map(
        shards, mesh=mesh, in_specs=placed, out_specs=P("wide", "narrow"), check_vma=False
    )
```
